32 devices in a mesh: ctx: 8 (over z, y), tp: 4 (over x, core).
Axes of the slice: x: 2, y: 2, z: 4, core: 2. Of those that a mesh axis runs over, the one named last changes fastest.
Arguments:
- outer_gate: bfloat16 [1024, 1024], P('ctx', 'tp'), may hold values from -6 to 6
- inner_gate: bfloat16 [1024, 1024], P('ctx', 'tp'), may hold values from -6 to 6
- values: bfloat16 [1024, 1024], P('ctx', 'tp'), may hold values from -6 to 6
- residues: float32 [16, 1024], P(None, 'tp'), may hold values from -4 to 4
- log_decay: float32 [16, 1024], P(None, 'tp'), may hold values from -16 to -2, as said below
- skip_gain: float32 [1024], P('tp'), may hold values from 0.5 to 1.5
- out_weight: bfloat16 [1024, 8192], P('tp'), may hold values from -0.25 to 0.25
- out_grad: bfloat16 [1024, 8192], P('ctx', 'tp'), may hold values from -1.5 to 1.5
Outputs:
- mixed: bfloat16 [1024, 8192], P('ctx', 'tp')
- grad_outer: bfloat16 [1024, 1024], P('ctx', 'tp')
- grad_inner: bfloat16 [1024, 1024], P('ctx', 'tp')
- grad_values: bfloat16 [1024, 1024], P('ctx', 'tp')
- grad_weight: float32 [1024, 8192], P('tp', 'ctx')
- grad_skip: float32 [1024], P('tp')
- grad_residues: float32 [16, 1024], P(None, 'tp')
- grad_decay: float32 [16, 1024], P(None, 'tp')
The draws below stay inside these ranges and needn't reach their ends.
Inputs may be any that keep to these rules, and one draw needn't show every extreme that they name: exp(log_decay) is a decay rate per position between 0.3 / 1024 and 0.12.
All inputs are finite; a program needn't handle non-finite values.
Results may differ from the reference program's by a relative error of at most 0.015.
Values may be sent and summed in bfloat16 or wider, within the bound.
A program may use at most 128 MiB of HBM per device.

```python
import jax
import jax.numpy as jnp
from jax import lax

D = 8192
C = 1024
MODES = 16
LENGTH = 1024


def draw_log_decay(key, part):
    key_slow, key_fast, key_pick = jax.random.split(key, 3)
    tokens_all = 1.0 * LENGTH
    slow_part = jax.random.uniform(key_slow, (MODES, C), jnp.float32, jnp.log(0.3 / tokens_all), jnp.log(2.0 / tokens_all))
    fast_part = jax.random.uniform(key_fast, (MODES, C), jnp.float32, jnp.log(0.04), jnp.log(0.12))
    slow_share = 0.5
    chosen = jax.random.uniform(key_pick, (MODES, C), jnp.float32) < slow_share
    return jnp.where(chosen, slow_part, fast_part)


def with_spikes(drawn, rng, source, target, blocks, factor):
    owner, partner = [(jnp.arange(drawn.shape[position]) // (drawn.shape[position] // blocks)).reshape([-1 if axis == position else 1 for axis in range(drawn.ndim)]) for position in (source, target)]
    chosen = jax.random.permutation(rng, blocks)[partner]
    strong = (owner == chosen) | (owner == (partner + blocks // 2) % blocks)
    return jnp.where(strong, factor * drawn, drawn)


def level_of(key, shape, pieces, smallest, largest):
    gain, own = 1.0, jax.random.fold_in(key, 6)
    for axis_at, shards_of in pieces:
        steps = jnp.exp(jax.random.uniform(jax.random.fold_in(own, axis_at), (shards_of,), jnp.float32, smallest / len(pieces), largest / len(pieces)))
        gain = gain * jnp.repeat(steps, shape[axis_at] // shards_of).reshape([-1 if axis == axis_at else 1 for axis in range(len(shape))])
    return gain


def normal_values(rng, shape, width, most, shards=(), kind=jnp.bfloat16):
    values = jax.random.normal(rng, shape, jnp.float32) * width
    if len(shards) > 0:
        values = level_of(rng, shape, shards, -0.22, 0.18) * values
    return jnp.clip(values, min=-most, max=most).astype(kind)


def gaussian_with(rng, dims, deviation, reach, cuts, heavy, held_as=jnp.bfloat16):
    values = deviation * jax.random.normal(rng, dims, jnp.float32)
    if cuts:
        values = values * level_of(rng, dims, cuts, -0.22, 0.18)
    return jnp.clip(with_spikes(values, jax.random.fold_in(rng, 3), *heavy), -reach, reach).astype(held_as)


def setup_inputs(seed: int = 0) -> dict:
    keys = jax.random.split(jax.random.key(seed), 9)
    outer_gate = normal_values(keys[0], (LENGTH, C), 1.0, 6.0, ((0, 8), (1, 4)))
    inner_gate = normal_values(keys[1], (LENGTH, C), 1.0, 6.0, ((0, 8), (1, 4)))
    values = normal_values(keys[2], (LENGTH, C), 1.0, 6.0, ((0, 8), (1, 4)))
    residues = normal_values(keys[3], (MODES, C), 0.25, 4.0, ((1, 4),), jnp.float32)
    log_decay = draw_log_decay(jax.random.fold_in(keys[8], 71), 0)
    skip_gain = jnp.clip(0.5 + 1.0 * jax.random.uniform(keys[5], (C,), jnp.float32) ** level_of(keys[5], (C,), ((0, 4),), -0.2, 0.2), 0.5, 1.5)
    out_weight = gaussian_with(keys[6], (C, D), C ** -0.5, 0.25, ((0, 4),), (0, 1, 4, 2.0))
    out_grad = gaussian_with(keys[7], (LENGTH, D), 0.25, 1.5, ((0, 8), (1, 4)), (0, 1, 8, 2.0))
    return dict(outer_gate=outer_gate, inner_gate=inner_gate, values=values, residues=residues, log_decay=log_decay, skip_gain=skip_gain, out_weight=out_weight, out_grad=out_grad)


def mode_rows(residue_row, decay_row, offsets):
    rate_row = jnp.exp(decay_row)
    gain_row = residue_row * jnp.sqrt(-jnp.expm1(-2.0 * rate_row))
    return gain_row[None, :] * jnp.exp(-rate_row[None, :] * offsets[:, None])

def impulse(residues, log_decay, offsets):

    def accumulate(summed, mode_pair):
        return (summed + mode_rows(mode_pair[0], mode_pair[1], offsets), None)
    initial = jnp.zeros((offsets.shape[0], residues.shape[1]), residues.dtype)
    summed, _ = lax.scan(accumulate, initial, (residues, log_decay))
    return summed

def impulse_grads(residues, log_decay, offsets, grad_response):

    def one_mode(carry, mode_pair):

        def rows_of(residue_row, decay_row):
            return mode_rows(residue_row, decay_row, offsets)
        _, pullback = jax.vjp(rows_of, mode_pair[0], mode_pair[1])
        grad_res, grad_dec = pullback(grad_response)
        return (carry, (grad_res, grad_dec))
    _, grads = lax.scan(one_mode, 0, (residues, log_decay))
    return grads

def reference(outer_gate, inner_gate, values, residues, log_decay, skip_gain, out_weight, out_grad):
    outer_f = outer_gate.astype(jnp.float32)
    inner_f = inner_gate.astype(jnp.float32)
    value_f = values.astype(jnp.float32)
    mixed_in = inner_f * value_f
    offsets = jnp.arange(LENGTH).astype(residues.dtype)
    response = impulse(residues, log_decay, offsets)
    padded_len = 2 * LENGTH
    spec_u = jnp.fft.rfft(mixed_in, n=padded_len, axis=0)
    spec_h = jnp.fft.rfft(response, n=padded_len, axis=0)
    conv_out = jnp.fft.irfft(spec_u * spec_h, n=padded_len, axis=0)[:LENGTH]
    gated = conv_out + skip_gain[None, :] * mixed_in
    result = (outer_f * gated).astype(jnp.bfloat16)
    mixed = jnp.dot(result, out_weight, preferred_element_type=jnp.float32).astype(jnp.bfloat16)
    grad_gated = jnp.dot(out_grad, out_weight.T, preferred_element_type=jnp.float32)
    grad_weight = jnp.dot(result.T, out_grad, preferred_element_type=jnp.float32)
    grad_conv = grad_gated * outer_f
    grad_outer = (grad_gated * gated).astype(jnp.bfloat16)
    spec_g = jnp.fft.rfft(grad_conv, n=padded_len, axis=0)
    corr_in = jnp.fft.irfft(spec_g * jnp.conj(spec_h), n=padded_len, axis=0)[:LENGTH]
    grad_mixed = corr_in + skip_gain[None, :] * grad_conv
    grad_inner = (grad_mixed * value_f).astype(jnp.bfloat16)
    grad_values = (grad_mixed * inner_f).astype(jnp.bfloat16)
    grad_skip = lax.optimization_barrier(jnp.sum(grad_conv * mixed_in, axis=0))
    grad_response = jnp.fft.irfft(spec_g * jnp.conj(spec_u), n=padded_len, axis=0)[:LENGTH]
    grad_residues, grad_decay = impulse_grads(residues, log_decay, offsets, grad_response)
    return (mixed, grad_outer, grad_inner, grad_values, grad_weight, grad_skip, grad_residues, grad_decay)
```

```python
import functools
import math

import jax
import jax.numpy as jnp
from jax import lax
from jax.experimental import pallas as pl
from jax.experimental.pallas import tpu as pltpu
from jax.sharding import PartitionSpec as P

PRECISE = lax.Precision.HIGHEST


def for_sending(array):
    return jax.tree.map(lambda a: a.astype(jnp.bfloat16) if a.dtype == jnp.float32 else a, array)


def reversed_bits(position, levels):
    result = position * 0
    for bit_place in range(levels):
        result = result * 2 + position // 2**bit_place % 2
    return result


def rotate(stacked, cosine, sine_part):
    return jnp.stack(
        [
            stacked[:, 0] * cosine - stacked[:, 1] * sine_part,
            stacked[:, 0] * sine_part + stacked[:, 1] * cosine,
        ],
        axis=1,
    )


def square_table(length_dev, flip_sign):
    indices = jnp.arange(length_dev, dtype=jnp.int32)
    products = indices[:, None] * indices[None, :] % length_dev
    angles = flip_sign * 2.0 * math.pi / length_dev * products.astype(jnp.float32)
    return (jnp.cos(angles), jnp.sin(angles))


def local_transform(stacked, flip_sign):
    cosine, sine_part = square_table(stacked.shape[2], flip_sign)
    real_part = jnp.einsum("ki,sic->skc", cosine, stacked[:, 0], precision=PRECISE) - jnp.einsum(
        "ki,sic->skc", sine_part, stacked[:, 1], precision=PRECISE
    )
    imag_part = jnp.einsum("ki,sic->skc", cosine, stacked[:, 1], precision=PRECISE) + jnp.einsum(
        "ki,sic->skc", sine_part, stacked[:, 0], precision=PRECISE
    )
    return jnp.stack([real_part, imag_part], axis=1)


def shift_table(device, levels, length_dev, length, flip_sign):
    low_index = reversed_bits(device, levels)
    indices = jnp.arange(length_dev, dtype=jnp.int32)
    products = indices * low_index % length
    angles = flip_sign * 2.0 * math.pi / length * products.astype(jnp.float32)
    return (jnp.cos(angles)[:, None], jnp.sin(angles)[:, None])


def device_table(levels, forward):
    ctx_size = 2**levels
    indices = jnp.arange(ctx_size, dtype=jnp.int32)
    flipped = reversed_bits(indices, levels)
    if forward:
        products = flipped[:, None] * indices[None, :]
        flip_sign = -1.0
    else:
        products = indices[:, None] * flipped[None, :]
        flip_sign = 1.0
    angles = flip_sign * 2.0 * math.pi / ctx_size * (products % ctx_size).astype(jnp.float32)
    return (jnp.cos(angles), jnp.sin(angles))


def transpose_transform(stacked, tables):
    cosine, sine_part = tables
    shaped = stacked.reshape(stacked.shape[0], 2, 1, stacked.shape[2], stacked.shape[3])
    blocks = lax.all_to_all(
        for_sending(shaped), "ctx", split_axis=3, concat_axis=2, tiled=True
    ).astype(shaped.dtype)
    real_part = jnp.einsum("pq,sqic->spic", cosine, blocks[:, 0], precision=PRECISE) - jnp.einsum(
        "pq,sqic->spic", sine_part, blocks[:, 1], precision=PRECISE
    )
    imag_part = jnp.einsum("pq,sqic->spic", cosine, blocks[:, 1], precision=PRECISE) + jnp.einsum(
        "pq,sqic->spic", sine_part, blocks[:, 0], precision=PRECISE
    )
    combined = jnp.stack([real_part, imag_part], axis=1)
    result = lax.all_to_all(
        for_sending(combined), "ctx", split_axis=2, concat_axis=3, tiled=True
    ).astype(combined.dtype)
    return result.reshape(stacked.shape)


def branch_phase(device, length_dev, length, flip_sign):
    positions = (device * length_dev + jnp.arange(length_dev, dtype=jnp.int32)).astype(jnp.float32)
    angles = flip_sign * math.pi / length * positions
    return (jnp.cos(angles)[:, None], jnp.sin(angles)[:, None])


def to_spectrum(signals, device, levels, length, across):
    length_dev = signals.shape[1]
    cosine, sine_part = branch_phase(device, length_dev, length, -1.0)
    zero_part = jnp.zeros_like(signals)
    even_part = jnp.stack([signals, zero_part], axis=1)
    odd_part = jnp.stack([signals * cosine, signals * sine_part], axis=1)
    stacked = jnp.concatenate([even_part, odd_part], axis=0)
    stacked = across(stacked, True)
    cosine, sine_part = shift_table(device, levels, length_dev, length, -1.0)
    stacked = rotate(stacked, cosine, sine_part)
    return local_transform(stacked, -1.0)


def from_spectrum(stacked, device, levels, length, across):
    length_dev = stacked.shape[2]
    stacked = local_transform(stacked, 1.0)
    cosine, sine_part = shift_table(device, levels, length_dev, length, 1.0)
    stacked = rotate(stacked, cosine, sine_part)
    stacked = across(stacked, False)
    half_count = stacked.shape[0] // 2
    lower_half = stacked[:half_count]
    upper_half = stacked[half_count:]
    cosine, sine_part = branch_phase(device, length_dev, length, 1.0)
    summed = lower_half[:, 0] + upper_half[:, 0] * cosine - upper_half[:, 1] * sine_part
    return summed / (2.0 * length)


def filter_spectrum(residues, log_decay, device, levels, length):
    ctx_size = 2**levels
    length_dev = length // ctx_size
    rate_rows = jnp.exp(log_decay)
    gain_rows = residues * jnp.sqrt(-jnp.expm1(-2.0 * rate_rows))
    falloff = jnp.exp(-rate_rows)[:, None, :]
    tail_part = jnp.exp(-rate_rows * length)
    rim_term = (-jnp.expm1(-rate_rows))[:, None, :]
    low_index = reversed_bits(device, levels)
    indices = jnp.arange(length_dev, dtype=jnp.int32)
    filters = []
    for branch in range(2):
        frequency = 2 * (low_index + ctx_size * indices) + branch
        phases = math.pi / length * frequency.astype(jnp.float32)
        sine_theta = jnp.sin(phases)[None, :, None]
        half_sine = jnp.sin(0.5 * phases)[None, :, None]
        denom_real = rim_term + falloff * 2.0 * half_sine * half_sine
        denom_imag = falloff * sine_theta
        if branch == 0:
            numerator = gain_rows * (1.0 - tail_part)
        else:
            numerator = gain_rows * (1.0 + tail_part)
        weighting = numerator[:, None, :] / (denom_real * denom_real + denom_imag * denom_imag)
        real_part = jnp.sum(weighting * denom_real, axis=0)
        imag_part = -jnp.sum(weighting * denom_imag, axis=0)
        filters.append(jnp.stack([real_part, imag_part], axis=0))
    return filters


def multiply(left_factor, right_factor, conjugate):
    flip_sign = -1.0 if conjugate else 1.0
    right_imag = flip_sign * right_factor[1]
    return jnp.stack(
        [
            left_factor[0] * right_factor[0] - left_factor[1] * right_imag,
            left_factor[0] * right_imag + left_factor[1] * right_factor[0],
        ],
        axis=0,
    )


def filter_rows(residues, log_decay, positions):
    rate_rows = jnp.exp(log_decay)
    gain_rows = residues * jnp.sqrt(-jnp.expm1(-2.0 * rate_rows))
    return jnp.sum(
        gain_rows[:, None, :] * jnp.exp(-rate_rows[:, None, :] * positions[None, :, None]), axis=0
    )


def spectral_terms(mixed_in, grad_conv, residues, log_decay, device, levels, length, across):
    length_dev = mixed_in.shape[0]
    spectra = to_spectrum(jnp.stack([mixed_in, grad_conv], axis=0), device, levels, length, across)
    filters = filter_spectrum(residues, log_decay, device, levels, length)
    products = []
    for branch in range(2):
        spec_u = spectra[2 * branch]
        spec_g = spectra[2 * branch + 1]
        spec_h = filters[branch]
        products = products + [
            multiply(spec_u, spec_h, False),
            multiply(spec_g, spec_h, True),
            multiply(spec_g, spec_u, True),
        ]
    outcomes = from_spectrum(jnp.stack(products, axis=0), device, levels, length, across)
    positions = (device * length_dev + jnp.arange(length_dev, dtype=jnp.int32)).astype(jnp.float32)

    def local_rows(residue_part, decay_part):
        return filter_rows(residue_part, decay_part, positions)

    _, pullback = jax.vjp(local_rows, residues, log_decay)
    grad_res_part, grad_decay_part = pullback(outcomes[2])
    return (outcomes[0], outcomes[1], grad_res_part, grad_decay_part)


def spectral_body(outer_gate, inner_gate, values, residues, log_decay, skip_gain, out_weight, out_grad):
    ctx_size = lax.axis_size("ctx")
    device = lax.axis_index("ctx")
    levels = ctx_size.bit_length() - 1
    length_dev = outer_gate.shape[0]
    length = ctx_size * length_dev
    outer_f = outer_gate.astype(jnp.float32)
    inner_f = inner_gate.astype(jnp.float32)
    value_f = values.astype(jnp.float32)
    mixed_in = inner_f * value_f
    full_grad = lax.all_gather(out_grad, "tp", axis=1, tiled=True)
    grad_gated = lax.dot_general(
        full_grad, out_weight, (((1,), (1,)), ((), ())), preferred_element_type=jnp.float32
    )
    grad_conv = grad_gated * outer_f

    def across(stacked, forward):
        return transpose_transform(stacked, device_table(levels, forward))

    conv_out, corr_in, grad_res_part, grad_decay_part = spectral_terms(
        mixed_in, grad_conv, residues, log_decay, device, levels, length, across
    )
    gated = conv_out + skip_gain[None, :] * mixed_in
    result = (outer_f * gated).astype(jnp.bfloat16)
    proj_part = jnp.dot(result, out_weight, preferred_element_type=jnp.float32)
    mixed_out = lax.psum_scatter(
        proj_part.astype(jnp.bfloat16), "tp", scatter_dimension=1, tiled=True
    )
    weight_part = lax.dot_general(
        result, full_grad, (((0,), (0,)), ((), ())), preferred_element_type=jnp.float32
    )
    grad_weight = lax.psum_scatter(weight_part, "ctx", scatter_dimension=1, tiled=True)
    grad_outer = (grad_gated * gated).astype(jnp.bfloat16)
    grad_mixed = corr_in + skip_gain[None, :] * grad_conv
    grad_inner = (grad_mixed * value_f).astype(jnp.bfloat16)
    grad_values = (grad_mixed * inner_f).astype(jnp.bfloat16)
    skip_part = jnp.sum(grad_conv * mixed_in, axis=0)
    grad_skip, grad_residues, grad_decay = lax.psum(
        (skip_part, grad_res_part, grad_decay_part), "ctx"
    )
    return (
        mixed_out,
        grad_outer,
        grad_inner,
        grad_values,
        grad_weight,
        grad_skip,
        grad_residues,
        grad_decay,
    )


MESH = pl.DeviceIdType.MESH
SUB = 8
BF16 = jnp.bfloat16
F32 = jnp.float32


def fused_kernel(
    n_ctx,
    n_tp,
    outer_ref,
    inner_ref,
    value_ref,
    tab_ref,
    skip_ref,
    weight_hbm,
    grad_ref,
    mixed_ref,
    gouter_ref,
    ginner_ref,
    gvalue_ref,
    gweight_ref,
    gskip_ref,
    gres_ref,
    gdec_ref,
    w_ref,
    og,
    og_t,
    res_all,
    st1,
    st2,
    d_cross,
    d_own,
    sib_out,
    sib_in,
    x_out,
    x_in,
    u_ref,
    y_ref,
    gg_ref,
    gc_ref,
    turn_ref,
    u_sub,
    gc_sub,
    rows,
    pre,
    pre2,
    w_sem,
    a_send,
    a_recv,
    t_send,
    t_recv,
    f_send,
    f_recv,
    e_send,
    e_recv,
    r_send,
    r_recv,
    g_send,
    g_recv,
    m_send,
    m_recv,
):
    c = lax.axis_index("ctx")
    t = lax.axis_index("tp")
    core = t % 2
    sib = t + 1 - 2 * core
    far = (t + 2) % n_tp
    far_sib = (sib + 2) % n_tp
    base = t - core
    n_rows, feats = grad_ref.shape
    chans = outer_ref.shape[1]
    modes = tab_ref.shape[0] // 8
    steps = n_rows // SUB
    block = feats * n_tp // n_ctx
    half = block // 2
    per = n_ctx // n_tp

    def remote(src, dst, send, recv, ctx_id, tp_id):
        return pltpu.make_async_remote_copy(
            src_ref=src,
            dst_ref=dst,
            send_sem=send,
            recv_sem=recv,
            device_id=(ctx_id, tp_id),
            device_id_type=MESH,
        )

    w_copy = pltpu.make_async_copy(weight_hbm, w_ref, w_sem)
    w_copy.start()

    barrier = pltpu.get_barrier_semaphore()

    def greet(d, carry):
        peer = (c + d) % n_ctx
        for h in range(2):
            pl.semaphore_signal(barrier, inc=1, device_id=(peer, base + h), device_id_type=MESH)
        return carry

    lax.fori_loop(1, n_ctx, greet, 0)
    pl.semaphore_signal(barrier, inc=1, device_id=(c, sib), device_id_type=MESH)
    pl.semaphore_signal(barrier, inc=1, device_id=(c, far), device_id_type=MESH)

    u_ref[...] = inner_ref[...].astype(F32) * value_ref[...].astype(F32)

    def table(which, n):
        return tab_ref[pl.ds(which * modes + n, 1), :]

    lanes = turn_ref.shape[2]

    def spread(value, ref):
        for k in range(chans // lanes):
            turn_ref[k] = value[:, k * lanes : (k + 1) * lanes]
        for i in range(steps):
            for k in range(chans // lanes):
                ref[i, :, k * lanes : (k + 1) * lanes] = turn_ref[k, pl.ds(i, SUB, stride=steps), :]

    def gathered(parts):
        for i in range(steps):
            for k in range(chans // lanes):
                turn_ref[k, pl.ds(i, SUB, stride=steps), :] = parts[i][:, k * lanes : (k + 1) * lanes]
        return jnp.concatenate([turn_ref[k] for k in range(chans // lanes)], axis=1)

    place = lax.broadcasted_iota(jnp.int32, (SUB, chans), 0)

    def down(x, k):
        return jnp.where(place >= k, pltpu.roll(x, k, 0), 0.0)

    def up(x, k):
        return jnp.where(place < SUB - k, pltpu.roll(x, SUB - k, 0), 0.0)

    spread(u_ref[...], u_sub)

    def first_states(n, carry):
        a = jnp.broadcast_to(table(0, n), (SUB, chans))
        q = jnp.broadcast_to(table(1, n), (SUB, chans))
        x = jnp.zeros((SUB, chans), F32)
        xp = jnp.zeros((SUB, chans), F32)
        for i in range(steps):
            xp = a * (xp + x)
            x = a * x + u_sub[i]
        k = 1
        while k < SUB:
            xs = down(x, k)
            xp = xp + q * (down(xp, k) + (1.0 * k * steps) * xs)
            x = x + q * xs
            q = q * q
            k *= 2
        pre[n] = down(x, 1)
        pre2[n] = down(xp, 1)
        rows[pl.ds(n, 1), :] = x[SUB - 1 :]
        rows[pl.ds(modes + n, 1), :] = xp[SUB - 1 :]
        return carry

    pl.semaphore_wait(barrier, 2 * n_ctx)

    pieces = per
    width = feats // pieces
    og[t] = grad_ref[...]

    def block_copies(b, slot, dst_tp):
        return [
            remote(
                og.at[b, :, pl.ds(p * width, width)],
                og.at[b, :, pl.ds(p * width, width)],
                a_send.at[slot, p],
                a_recv.at[slot, p],
                c,
                dst_tp,
            )
            for p in range(pieces)
        ]

    def turned(b, slot, j, h):
        return remote(
            og.at[b, :, pl.ds(j * block + h * half, half)],
            og_t.at[h, c],
            t_send.at[slot, j, h],
            t_recv.at[c],
            per * b + j,
            base + h,
        )

    def start_turned(b, slot, j):
        @pl.when(per * b + j != c)
        def _():
            for h in range(2):
                turned(b, slot, j, h).start()

    to_far = block_copies(t, 0, far)
    to_sib = block_copies(t, 1, sib)
    for cp in to_far:
        cp.start()
    for cp in to_sib:
        cp.start()

    lax.fori_loop(0, modes, first_states, 0)
    st1[c] = rows[: 2 * modes, :].astype(BF16)

    def e_copy(d):
        return remote(
            st1.at[c], st1.at[c], e_send.at[d], e_recv.at[d], (c + d) % n_ctx, t
        )

    def each_peer(action):
        def step(d, carry):
            action(d)
            return carry

        lax.fori_loop(1, n_ctx, step, 0)

    each_peer(lambda d: e_copy(d).start())
    for j in range(per):
        start_turned(t, 0, j)

    def e_wait(d):
        slot = (c + n_ctx - d) % n_ctx
        remote(st1.at[slot], st1.at[slot], e_send.at[d], e_recv.at[d], c, t).wait_recv()

    each_peer(e_wait)

    q_dev = tab_ref[2 * modes : 3 * modes, :]

    def chain(k, carry):
        x, xp = carry
        block_state = st1[k].astype(F32)
        keep = k < c
        xp_new = q_dev * (xp + (1.0 * n_rows) * x) + block_state[modes:]
        x_new = q_dev * x + block_state[:modes]
        return jnp.where(keep, x_new, x), jnp.where(keep, xp_new, xp)

    zero = jnp.zeros((modes, chans), F32)
    x_in_state, xp_in_state = lax.fori_loop(0, n_ctx, chain, (zero, zero))
    rows[:modes, :] = x_in_state
    rows[modes : 2 * modes, :] = xp_in_state
    offset = (place * steps).astype(F32)

    def second(n, carry):
        a = jnp.broadcast_to(table(0, n), (SUB, chans))
        gain = jnp.broadcast_to(table(3, n), (SUB, chans))
        fade = jnp.exp(-offset * table(4, n))
        x0 = rows[pl.ds(n, 1), :]
        xp0 = rows[pl.ds(modes + n, 1), :]
        x = pre[n] + fade * x0
        xp = pre2[n] + fade * (xp0 + offset * x0)
        pre[n] = x
        pre2[n] = xp
        out = []
        for i in range(steps):
            x = a * x + u_sub[i]
            out.append(carry[i] + gain * x)
        return tuple(out)

    ys = lax.fori_loop(
        0, modes, second, tuple(jnp.zeros((SUB, chans), F32) for _ in range(steps))
    )
    y_ref[...] = gathered(ys) + skip_ref[...] * u_ref[...]

    res_all[c] = (outer_ref[...].astype(F32) * y_ref[...]).astype(BF16)

    def r_copy(d):
        return remote(
            res_all.at[c], res_all.at[c], r_send.at[d], r_recv.at[d], (c + d) % n_ctx, t
        )

    each_peer(lambda d: r_copy(d).start())

    w_copy.wait()
    tile = min(512, feats)

    def project(dest, sink):
        def step(k, carry):
            col = pl.multiple_of(k * tile, tile)
            part = jnp.dot(
                res_all[c],
                w_ref[:, pl.ds(pl.multiple_of(dest * feats + col, tile), tile)],
                preferred_element_type=F32,
            )
            sink[:, pl.ds(col, tile)] = part.astype(sink.dtype)
            return carry

        lax.fori_loop(0, feats // tile, step, 0)

    m_sib = [
        remote(sib_out.at[k], sib_in.at[k], m_send.at[k], m_recv.at[k], c, sib) for k in range(2)
    ]
    m_far = remote(x_out, x_in, m_send.at[2], m_recv.at[2], c, far)

    project(far_sib, sib_out.at[0])
    m_sib[0].start()
    project(far, d_cross)

    far_in = block_copies(far, 0, far)
    fwd = block_copies(far, 2, sib)
    for p in range(pieces):
        far_in[p].wait_recv()
        fwd[p].start()
        start_turned(far, 1, p)

    m_sib[0].wait_recv()
    x_out[...] = (d_cross[...] + sib_in[0].astype(F32)).astype(BF16)
    m_far.start()

    project(sib, sib_out.at[1])
    m_sib[1].start()
    project(t, d_own)

    for p in range(pieces):
        block_copies(sib, 1, sib)[p].wait_recv()
    for p in range(pieces):
        block_copies(far_sib, 2, sib)[p].wait_recv()

    gg_ref[...] = jnp.zeros_like(gg_ref)

    def back_project(b, carry):
        for k in range(feats // tile):
            gg_ref[...] += lax.dot_general(
                og[b, :, pl.ds(k * tile, tile)],
                w_ref[:, pl.ds(pl.multiple_of(b * feats + k * tile, tile), tile)],
                (((1,), (1,)), ((), ())),
                preferred_element_type=F32,
            )
        return carry

    lax.fori_loop(0, n_tp, back_project, 0)
    gc_ref[...] = gg_ref[...] * outer_ref[...].astype(F32)
    gouter_ref[...] = (gg_ref[...] * y_ref[...]).astype(BF16)

    spread(gc_ref[...], gc_sub)

    def third(n, carry):
        a = jnp.broadcast_to(table(0, n), (SUB, chans))
        q = jnp.broadcast_to(table(1, n), (SUB, chans))
        x = pre[n]
        xp = pre2[n]
        sum_a = jnp.zeros((SUB, chans), F32)
        sum_b = jnp.zeros((SUB, chans), F32)
        w = jnp.zeros((SUB, chans), F32)
        for i in range(steps):
            g = gc_sub[i]
            xp = a * (xp + x)
            x = a * x + u_sub[i]
            sum_a = sum_a + g * x
            sum_b = sum_b + g * xp
            w = a * w + gc_sub[steps - 1 - i]
        k = 1
        while k < SUB:
            w = w + q * up(w, k)
            q = q * q
            k *= 2
        pre[n] = up(w, 1)
        rows[pl.ds(n, 1), :] = w[:1]
        rows[pl.ds(modes + n, 1), :] = jnp.sum(sum_a, axis=0, keepdims=True)
        rows[pl.ds(2 * modes + n, 1), :] = jnp.sum(sum_b, axis=0, keepdims=True)
        return carry

    lax.fori_loop(0, modes, third, 0)
    rows[3 * modes :, :] = jnp.broadcast_to(
        jnp.sum(gc_ref[...] * u_ref[...], axis=0, keepdims=True), (modes, chans)
    )
    st2[c] = rows[...].astype(BF16)

    def g_copy(d):
        return remote(
            st2.at[c], st2.at[c], g_send.at[d], g_recv.at[d], (c + d) % n_ctx, t
        )

    each_peer(lambda d: g_copy(d).start())

    m_sib[1].wait_recv()
    d_own[...] += sib_in[1].astype(F32)
    m_far.wait_recv()
    mixed_ref[...] = (d_own[...] + x_in[...].astype(F32)).astype(BF16)

    def g_wait(d):
        slot = (c + n_ctx - d) % n_ctx
        remote(st2.at[slot], st2.at[slot], g_send.at[d], g_recv.at[d], c, t).wait_recv()

    each_peer(g_wait)

    def chain_back(k, carry):
        w, total = carry
        dev = n_ctx - 1 - k
        state = st2[dev].astype(F32)
        return (
            jnp.where(dev > c, q_dev * w + state[:modes], w),
            total + state[modes:],
        )

    w_state, total = lax.fori_loop(
        0, n_ctx, chain_back, (zero, jnp.zeros((3 * modes, chans), F32))
    )
    rows[:modes, :] = w_state
    fac = tab_ref[5 * modes : 6 * modes, :]
    gres_ref[...] = fac * total[:modes]
    gdec_ref[...] = (
        tab_ref[6 * modes : 7 * modes, :] * total[:modes]
        - tab_ref[7 * modes :, :] * total[modes : 2 * modes]
    )
    gskip_ref[...] = total[2 * modes : 2 * modes + 1]

    back_offset = ((SUB - 1 - place) * steps).astype(F32)

    def fourth(n, carry):
        a = jnp.broadcast_to(table(0, n), (SUB, chans))
        gain = jnp.broadcast_to(table(3, n), (SUB, chans))
        w = pre[n] + jnp.exp(-back_offset * table(4, n)) * rows[pl.ds(n, 1), :]
        out = []
        for i in range(steps):
            w = a * w + gc_sub[steps - 1 - i]
            out.append(carry[i] + gain * w)
        return tuple(out)

    ws = lax.fori_loop(
        0, modes, fourth, tuple(jnp.zeros((SUB, chans), F32) for _ in range(steps))
    )
    y_ref[...] = gathered(ws[::-1]) + skip_ref[...] * gc_ref[...]
    ginner_ref[...] = (y_ref[...] * value_ref[...].astype(F32)).astype(BF16)
    gvalue_ref[...] = (y_ref[...] * inner_ref[...].astype(F32)).astype(BF16)

    own_b = c // per
    own_j = c % per
    for h in range(2):
        og_t[h, c] = og[own_b, :, pl.ds(pl.multiple_of(own_j * block + h * half, half), half)]

    def f_copy(slot, h):
        return remote(
            og_t.at[h, slot], og_t.at[h, slot], f_send.at[slot], f_recv.at[slot], c, sib
        )

    def pass_on(d):
        slot = (c + n_ctx - d) % n_ctx
        remote(
            og_t.at[core, slot], og_t.at[core, slot], t_send.at[0, 0, 0], t_recv.at[slot], c, t
        ).wait_recv()
        f_copy(slot, core).start()

    each_peer(pass_on)

    def r_wait(d):
        slot = (c + n_ctx - d) % n_ctx
        remote(
            res_all.at[slot], res_all.at[slot], r_send.at[d], r_recv.at[d], c, t
        ).wait_recv()

    each_peer(r_wait)

    def weigh(h):
        left = res_all[...].reshape(n_ctx * n_rows, chans)
        right = og_t[h].reshape(n_ctx * n_rows, half)
        gweight_ref[:, pl.ds(pl.multiple_of(h * half, half), half)] = lax.dot_general(
            left, right, (((0,), (0,)), ((), ())), preferred_element_type=F32
        )

    weigh(core)

    def f_wait(d):
        slot = (c + n_ctx - d) % n_ctx
        f_copy(slot, 1 - core).wait_recv()

    each_peer(f_wait)
    weigh(1 - core)

    for cp in to_far + to_sib + fwd:
        cp.wait_send()
    for slot, b in enumerate((t, far)):
        for j in range(per):

            @pl.when(per * b + j != c)
            def _():
                for h in range(2):
                    turned(b, slot, j, h).wait_send()

    def sent(d):
        slot = (c + n_ctx - d) % n_ctx
        f_copy(slot, core).wait_send()
        e_copy(d).wait_send()
        r_copy(d).wait_send()
        g_copy(d).wait_send()

    each_peer(sent)
    for cp in m_sib + [m_far]:
        cp.wait_send()


def fused_body(
    n_ctx, n_tp, outer_gate, inner_gate, values, residues, log_decay, skip_gain, out_weight, out_grad
):
    n_rows, chans = outer_gate.shape
    feats = out_grad.shape[1]
    modes = residues.shape[0]
    steps = n_rows // SUB
    block = feats * n_tp // n_ctx
    per = n_ctx // n_tp
    rate = jnp.exp(log_decay)
    fac = jnp.sqrt(-jnp.expm1(-2.0 * rate))
    tables = jnp.concatenate(
        [
            jnp.exp(-rate),
            jnp.exp(-rate * steps),
            jnp.exp(-rate * n_rows),
            residues * fac,
            rate,
            fac,
            rate * residues * jnp.exp(-2.0 * rate) / fac,
            rate * residues * fac,
        ],
        axis=0,
    )
    vmem = pl.BlockSpec(memory_space=pltpu.VMEM)
    dma = pltpu.SemaphoreType.DMA
    outs = pl.pallas_call(
        functools.partial(fused_kernel, n_ctx, n_tp),
        out_shape=(
            jax.ShapeDtypeStruct((n_rows, feats), BF16),
            jax.ShapeDtypeStruct((n_rows, chans), BF16),
            jax.ShapeDtypeStruct((n_rows, chans), BF16),
            jax.ShapeDtypeStruct((n_rows, chans), BF16),
            jax.ShapeDtypeStruct((chans, block), F32),
            jax.ShapeDtypeStruct((1, chans), F32),
            jax.ShapeDtypeStruct((modes, chans), F32),
            jax.ShapeDtypeStruct((modes, chans), F32),
        ),
        in_specs=[vmem] * 5 + [pl.BlockSpec(memory_space=pl.ANY), vmem],
        out_specs=(vmem,) * 8,
        scratch_shapes=[
            pltpu.VMEM(out_weight.shape, BF16),
            pltpu.VMEM((n_tp, n_rows, feats), BF16),
            pltpu.VMEM((2, n_ctx, n_rows, block // 2), BF16),
            pltpu.VMEM((n_ctx, n_rows, chans), BF16),
            pltpu.VMEM((n_ctx, 2 * modes, chans), BF16),
            pltpu.VMEM((n_ctx, 4 * modes, chans), BF16),
            pltpu.VMEM((n_rows, feats), F32),
            pltpu.VMEM((n_rows, feats), F32),
            pltpu.VMEM((2, n_rows, feats), BF16),
            pltpu.VMEM((2, n_rows, feats), BF16),
            pltpu.VMEM((n_rows, feats), BF16),
            pltpu.VMEM((n_rows, feats), BF16),
            pltpu.VMEM((n_rows, chans), F32),
            pltpu.VMEM((n_rows, chans), F32),
            pltpu.VMEM((n_rows, chans), F32),
            pltpu.VMEM((n_rows, chans), F32),
            pltpu.VMEM((chans // 128, n_rows, 128), F32),
            pltpu.VMEM((steps, SUB, chans), F32),
            pltpu.VMEM((steps, SUB, chans), F32),
            pltpu.VMEM((4 * modes, chans), F32),
            pltpu.VMEM((modes, SUB, chans), F32),
            pltpu.VMEM((modes, SUB, chans), F32),
            dma,
            dma((3, per)),
            dma((3, per)),
            dma((2, per, 2)),
            dma((n_ctx,)),
            dma((n_ctx,)),
            dma((n_ctx,)),
            dma((n_ctx,)),
            dma((n_ctx,)),
            dma((n_ctx,)),
            dma((n_ctx,)),
            dma((n_ctx,)),
            dma((n_ctx,)),
            dma((3,)),
            dma((3,)),
        ],
        compiler_params=pltpu.CompilerParams(
            collective_id=0, has_side_effects=True, vmem_limit_bytes=48 * 2**20
        ),
    )(outer_gate, inner_gate, values, tables, skip_gain[None, :], out_weight, out_grad)
    return outs[:5] + (outs[5][0],) + outs[6:]


def body(n_ctx, n_tp, *arrays):
    n_rows = arrays[0].shape[0]
    feats = arrays[-1].shape[1]
    modes = arrays[3].shape[0]
    pairs = n_tp == 4 and n_ctx % n_tp == 0 and (feats * n_tp // n_ctx) % 256 == 0
    if pairs and n_rows % 16 == 0 and modes % 16 == 0:
        return fused_body(n_ctx, n_tp, *arrays)
    return spectral_body(*arrays)


def solution(mesh):
    placed = (
        P("ctx", "tp"),
        P("ctx", "tp"),
        P("ctx", "tp"),
        P(None, "tp"),
        P(None, "tp"),
        P("tp"),
        P("tp", None),
        P("ctx", "tp"),
    )
    return jax.shard_map(
        functools.partial(body, mesh.shape["ctx"], mesh.shape["tp"]),
        mesh=mesh,
        in_specs=placed,
        out_specs=(
            P("ctx", "tp"),
            P("ctx", "tp"),
            P("ctx", "tp"),
            P("ctx", "tp"),
            P("tp", "ctx"),
            P("tp"),
            P(None, "tp"),
            P(None, "tp"),
        ),
        check_vma=False,
    )
```

```python
import functools
import math

import jax
import jax.numpy as jnp
from jax import lax
from jax.experimental import pallas as pl
from jax.experimental.pallas import tpu as pltpu
from jax.sharding import PartitionSpec as P

PRECISE = lax.Precision.HIGHEST


def for_sending(array):
    return jax.tree.map(lambda a: a.astype(jnp.bfloat16) if a.dtype == jnp.float32 else a, array)


def reversed_bits(position, levels):
    result = position * 0
    for bit_place in range(levels):
        result = result * 2 + position // 2**bit_place % 2
    return result


def rotate(stacked, cosine, sine_part):
    return jnp.stack(
        [
            stacked[:, 0] * cosine - stacked[:, 1] * sine_part,
            stacked[:, 0] * sine_part + stacked[:, 1] * cosine,
        ],
        axis=1,
    )


def square_table(length_dev, flip_sign):
    indices = jnp.arange(length_dev, dtype=jnp.int32)
    products = indices[:, None] * indices[None, :] % length_dev
    angles = flip_sign * 2.0 * math.pi / length_dev * products.astype(jnp.float32)
    return (jnp.cos(angles), jnp.sin(angles))


def local_transform(stacked, flip_sign):
    cosine, sine_part = square_table(stacked.shape[2], flip_sign)
    real_part = jnp.einsum("ki,sic->skc", cosine, stacked[:, 0], precision=PRECISE) - jnp.einsum(
        "ki,sic->skc", sine_part, stacked[:, 1], precision=PRECISE
    )
    imag_part = jnp.einsum("ki,sic->skc", cosine, stacked[:, 1], precision=PRECISE) + jnp.einsum(
        "ki,sic->skc", sine_part, stacked[:, 0], precision=PRECISE
    )
    return jnp.stack([real_part, imag_part], axis=1)


def shift_table(device, levels, length_dev, length, flip_sign):
    low_index = reversed_bits(device, levels)
    indices = jnp.arange(length_dev, dtype=jnp.int32)
    products = indices * low_index % length
    angles = flip_sign * 2.0 * math.pi / length * products.astype(jnp.float32)
    return (jnp.cos(angles)[:, None], jnp.sin(angles)[:, None])


def device_table(levels, forward):
    ctx_size = 2**levels
    indices = jnp.arange(ctx_size, dtype=jnp.int32)
    flipped = reversed_bits(indices, levels)
    if forward:
        products = flipped[:, None] * indices[None, :]
        flip_sign = -1.0
    else:
        products = indices[:, None] * flipped[None, :]
        flip_sign = 1.0
    angles = flip_sign * 2.0 * math.pi / ctx_size * (products % ctx_size).astype(jnp.float32)
    return (jnp.cos(angles), jnp.sin(angles))


def transpose_transform(stacked, tables):
    cosine, sine_part = tables
    shaped = stacked.reshape(stacked.shape[0], 2, 1, stacked.shape[2], stacked.shape[3])
    blocks = lax.all_to_all(
        for_sending(shaped), "ctx", split_axis=3, concat_axis=2, tiled=True
    ).astype(shaped.dtype)
    real_part = jnp.einsum("pq,sqic->spic", cosine, blocks[:, 0], precision=PRECISE) - jnp.einsum(
        "pq,sqic->spic", sine_part, blocks[:, 1], precision=PRECISE
    )
    imag_part = jnp.einsum("pq,sqic->spic", cosine, blocks[:, 1], precision=PRECISE) + jnp.einsum(
        "pq,sqic->spic", sine_part, blocks[:, 0], precision=PRECISE
    )
    combined = jnp.stack([real_part, imag_part], axis=1)
    result = lax.all_to_all(
        for_sending(combined), "ctx", split_axis=2, concat_axis=3, tiled=True
    ).astype(combined.dtype)
    return result.reshape(stacked.shape)


def branch_phase(device, length_dev, length, flip_sign):
    positions = (device * length_dev + jnp.arange(length_dev, dtype=jnp.int32)).astype(jnp.float32)
    angles = flip_sign * math.pi / length * positions
    return (jnp.cos(angles)[:, None], jnp.sin(angles)[:, None])


def to_spectrum(signals, device, levels, length, across):
    length_dev = signals.shape[1]
    cosine, sine_part = branch_phase(device, length_dev, length, -1.0)
    zero_part = jnp.zeros_like(signals)
    even_part = jnp.stack([signals, zero_part], axis=1)
    odd_part = jnp.stack([signals * cosine, signals * sine_part], axis=1)
    stacked = jnp.concatenate([even_part, odd_part], axis=0)
    stacked = across(stacked, True)
    cosine, sine_part = shift_table(device, levels, length_dev, length, -1.0)
    stacked = rotate(stacked, cosine, sine_part)
    return local_transform(stacked, -1.0)


def from_spectrum(stacked, device, levels, length, across):
    length_dev = stacked.shape[2]
    stacked = local_transform(stacked, 1.0)
    cosine, sine_part = shift_table(device, levels, length_dev, length, 1.0)
    stacked = rotate(stacked, cosine, sine_part)
    stacked = across(stacked, False)
    half_count = stacked.shape[0] // 2
    lower_half = stacked[:half_count]
    upper_half = stacked[half_count:]
    cosine, sine_part = branch_phase(device, length_dev, length, 1.0)
    summed = lower_half[:, 0] + upper_half[:, 0] * cosine - upper_half[:, 1] * sine_part
    return summed / (2.0 * length)


def filter_spectrum(residues, log_decay, device, levels, length):
    ctx_size = 2**levels
    length_dev = length // ctx_size
    rate_rows = jnp.exp(log_decay)
    gain_rows = residues * jnp.sqrt(-jnp.expm1(-2.0 * rate_rows))
    falloff = jnp.exp(-rate_rows)[:, None, :]
    tail_part = jnp.exp(-rate_rows * length)
    rim_term = (-jnp.expm1(-rate_rows))[:, None, :]
    low_index = reversed_bits(device, levels)
    indices = jnp.arange(length_dev, dtype=jnp.int32)
    filters = []
    for branch in range(2):
        frequency = 2 * (low_index + ctx_size * indices) + branch
        phases = math.pi / length * frequency.astype(jnp.float32)
        sine_theta = jnp.sin(phases)[None, :, None]
        half_sine = jnp.sin(0.5 * phases)[None, :, None]
        denom_real = rim_term + falloff * 2.0 * half_sine * half_sine
        denom_imag = falloff * sine_theta
        if branch == 0:
            numerator = gain_rows * (1.0 - tail_part)
        else:
            numerator = gain_rows * (1.0 + tail_part)
        weighting = numerator[:, None, :] / (denom_real * denom_real + denom_imag * denom_imag)
        real_part = jnp.sum(weighting * denom_real, axis=0)
        imag_part = -jnp.sum(weighting * denom_imag, axis=0)
        filters.append(jnp.stack([real_part, imag_part], axis=0))
    return filters


def multiply(left_factor, right_factor, conjugate):
    flip_sign = -1.0 if conjugate else 1.0
    right_imag = flip_sign * right_factor[1]
    return jnp.stack(
        [
            left_factor[0] * right_factor[0] - left_factor[1] * right_imag,
            left_factor[0] * right_imag + left_factor[1] * right_factor[0],
        ],
        axis=0,
    )


def filter_rows(residues, log_decay, positions):
    rate_rows = jnp.exp(log_decay)
    gain_rows = residues * jnp.sqrt(-jnp.expm1(-2.0 * rate_rows))
    return jnp.sum(
        gain_rows[:, None, :] * jnp.exp(-rate_rows[:, None, :] * positions[None, :, None]), axis=0
    )


def spectral_terms(mixed_in, grad_conv, residues, log_decay, device, levels, length, across):
    length_dev = mixed_in.shape[0]
    spectra = to_spectrum(jnp.stack([mixed_in, grad_conv], axis=0), device, levels, length, across)
    filters = filter_spectrum(residues, log_decay, device, levels, length)
    products = []
    for branch in range(2):
        spec_u = spectra[2 * branch]
        spec_g = spectra[2 * branch + 1]
        spec_h = filters[branch]
        products = products + [
            multiply(spec_u, spec_h, False),
            multiply(spec_g, spec_h, True),
            multiply(spec_g, spec_u, True),
        ]
    outcomes = from_spectrum(jnp.stack(products, axis=0), device, levels, length, across)
    positions = (device * length_dev + jnp.arange(length_dev, dtype=jnp.int32)).astype(jnp.float32)

    def local_rows(residue_part, decay_part):
        return filter_rows(residue_part, decay_part, positions)

    _, pullback = jax.vjp(local_rows, residues, log_decay)
    grad_res_part, grad_decay_part = pullback(outcomes[2])
    return (outcomes[0], outcomes[1], grad_res_part, grad_decay_part)


def spectral_body(outer_gate, inner_gate, values, residues, log_decay, skip_gain, out_weight, out_grad):
    ctx_size = lax.axis_size("ctx")
    device = lax.axis_index("ctx")
    levels = ctx_size.bit_length() - 1
    length_dev = outer_gate.shape[0]
    length = ctx_size * length_dev
    outer_f = outer_gate.astype(jnp.float32)
    inner_f = inner_gate.astype(jnp.float32)
    value_f = values.astype(jnp.float32)
    mixed_in = inner_f * value_f
    full_grad = lax.all_gather(out_grad, "tp", axis=1, tiled=True)
    grad_gated = lax.dot_general(
        full_grad, out_weight, (((1,), (1,)), ((), ())), preferred_element_type=jnp.float32
    )
    grad_conv = grad_gated * outer_f

    def across(stacked, forward):
        return transpose_transform(stacked, device_table(levels, forward))

    conv_out, corr_in, grad_res_part, grad_decay_part = spectral_terms(
        mixed_in, grad_conv, residues, log_decay, device, levels, length, across
    )
    gated = conv_out + skip_gain[None, :] * mixed_in
    result = (outer_f * gated).astype(jnp.bfloat16)
    proj_part = jnp.dot(result, out_weight, preferred_element_type=jnp.float32)
    mixed_out = lax.psum_scatter(
        proj_part.astype(jnp.bfloat16), "tp", scatter_dimension=1, tiled=True
    )
    weight_part = lax.dot_general(
        result, full_grad, (((0,), (0,)), ((), ())), preferred_element_type=jnp.float32
    )
    grad_weight = lax.psum_scatter(weight_part, "ctx", scatter_dimension=1, tiled=True)
    grad_outer = (grad_gated * gated).astype(jnp.bfloat16)
    grad_mixed = corr_in + skip_gain[None, :] * grad_conv
    grad_inner = (grad_mixed * value_f).astype(jnp.bfloat16)
    grad_values = (grad_mixed * inner_f).astype(jnp.bfloat16)
    skip_part = jnp.sum(grad_conv * mixed_in, axis=0)
    grad_skip, grad_residues, grad_decay = lax.psum(
        (skip_part, grad_res_part, grad_decay_part), "ctx"
    )
    return (
        mixed_out,
        grad_outer,
        grad_inner,
        grad_values,
        grad_weight,
        grad_skip,
        grad_residues,
        grad_decay,
    )


MESH = pl.DeviceIdType.MESH
SUB = 8
BF16 = jnp.bfloat16
F32 = jnp.float32


def fused_kernel(
    n_ctx,
    n_tp,
    outer_hbm,
    inner_hbm,
    value_hbm,
    res_hbm,
    dec_hbm,
    skip_hbm,
    weight_hbm,
    grad_hbm,
    mixed_ref,
    gouter_ref,
    ginner_ref,
    gvalue_ref,
    gweight_ref,
    gskip_ref,
    gres_ref,
    gdec_ref,
    outer_ref,
    inner_ref,
    value_ref,
    modal_ref,
    skip_ref,
    tab_ref,
    w_ref,
    og,
    og_t,
    res_all,
    st1,
    st2,
    d_cross,
    d_own,
    sib_out,
    sib_in,
    x_out,
    x_in,
    u_ref,
    y_ref,
    gg_ref,
    gc_ref,
    turn_ref,
    u_sub,
    gc_sub,
    rows,
    pre,
    pre2,
    in_sem,
    w_sem,
    a_send,
    a_recv,
    t_send,
    t_recv,
    f_send,
    f_recv,
    e_send,
    e_recv,
    r_send,
    r_recv,
    g_send,
    g_recv,
    m_send,
    m_recv,
):
    c = lax.axis_index("ctx")
    t = lax.axis_index("tp")
    core = t % 2
    sib = t + 1 - 2 * core
    far = (t + 2) % n_tp
    far_sib = (sib + 2) % n_tp
    base = t - core
    n_rows, feats = grad_hbm.shape
    chans = outer_ref.shape[1]
    modes = modal_ref.shape[1]
    steps = n_rows // SUB
    block = feats * n_tp // n_ctx
    share = block // n_tp
    per = n_ctx // n_tp

    def remote(src, dst, send, recv, ctx_id, tp_id):
        return pltpu.make_async_remote_copy(
            src_ref=src,
            dst_ref=dst,
            send_sem=send,
            recv_sem=recv,
            device_id=(ctx_id, tp_id),
            device_id_type=MESH,
        )

    w_copy = pltpu.make_async_copy(weight_hbm, w_ref, w_sem)
    loads = [
        pltpu.make_async_copy(src, dst, in_sem.at[k])
        for k, (src, dst) in enumerate(
            (
                (grad_hbm, og.at[t]),
                (dec_hbm, modal_ref.at[0]),
                (res_hbm, modal_ref.at[1]),
                (inner_hbm, inner_ref),
                (value_hbm, value_ref),
                (outer_hbm, outer_ref),
                (skip_hbm, skip_ref),
            )
        )
    ]
    for load in loads:
        load.start()

    barrier = pltpu.get_barrier_semaphore()

    def greet(d, carry):
        peer = (c + d) % n_ctx
        for h in range(2):
            pl.semaphore_signal(barrier, inc=1, device_id=(peer, base + h), device_id_type=MESH)
        return carry

    lax.fori_loop(1, n_ctx, greet, 0)
    pl.semaphore_signal(barrier, inc=1, device_id=(c, sib), device_id_type=MESH)
    pl.semaphore_signal(barrier, inc=1, device_id=(c, far), device_id_type=MESH)

    for load in loads[1:]:
        load.wait()
    w_copy.start()
    rate = jnp.exp(modal_ref[0])
    twice = 2.0 * rate
    series = twice * (
        1.0
        - twice / 2.0
        * (1.0 - twice / 3.0 * (1.0 - twice / 4.0 * (1.0 - twice / 5.0 * (1.0 - twice / 6.0 * (1.0 - twice / 7.0)))))
    )
    fac = jnp.sqrt(jnp.where(twice < 0.3, series, 1.0 - jnp.exp(-twice)))
    weighted = modal_ref[1] * fac
    for k, part in enumerate(
        (
            jnp.exp(-rate),
            jnp.exp(-rate * steps),
            jnp.exp(-rate * n_rows),
            weighted,
            rate,
            fac,
            rate * modal_ref[1] * jnp.exp(-twice) / fac,
            rate * weighted,
        )
    ):
        tab_ref[k * modes : (k + 1) * modes, :] = part

    u_ref[...] = inner_ref[...].astype(F32) * value_ref[...].astype(F32)

    def table(which, n):
        return tab_ref[pl.ds(which * modes + n, 1), :]

    lanes = turn_ref.shape[2]

    def spread(value, ref):
        for k in range(chans // lanes):
            turn_ref[k] = value[:, k * lanes : (k + 1) * lanes]
        for i in range(steps):
            for k in range(chans // lanes):
                ref[i, :, k * lanes : (k + 1) * lanes] = turn_ref[k, pl.ds(i, SUB, stride=steps), :]

    def gathered(parts):
        for i in range(steps):
            for k in range(chans // lanes):
                turn_ref[k, pl.ds(i, SUB, stride=steps), :] = parts[i][:, k * lanes : (k + 1) * lanes]
        return jnp.concatenate([turn_ref[k] for k in range(chans // lanes)], axis=1)

    place = lax.broadcasted_iota(jnp.int32, (SUB, chans), 0)

    def down(x, k):
        return jnp.where(place >= k, pltpu.roll(x, k, 0), 0.0)

    def up(x, k):
        return jnp.where(place < SUB - k, pltpu.roll(x, SUB - k, 0), 0.0)

    spread(u_ref[...], u_sub)

    def first_states(n, carry):
        a = jnp.broadcast_to(table(0, n), (SUB, chans))
        q = jnp.broadcast_to(table(1, n), (SUB, chans))
        x = jnp.zeros((SUB, chans), F32)
        xp = jnp.zeros((SUB, chans), F32)
        for i in range(steps):
            xp = a * (xp + x)
            x = a * x + u_sub[i]
        k = 1
        while k < SUB:
            xs = down(x, k)
            xp = xp + q * (down(xp, k) + (1.0 * k * steps) * xs)
            x = x + q * xs
            q = q * q
            k *= 2
        pre[n] = down(x, 1)
        pre2[n] = down(xp, 1)
        rows[pl.ds(n, 1), :] = x[SUB - 1 :]
        rows[pl.ds(modes + n, 1), :] = xp[SUB - 1 :]
        return carry

    pl.semaphore_wait(barrier, 2 * n_ctx)

    pieces = per
    width = feats // pieces
    loads[0].wait()

    def block_copies(b, slot, dst_tp):
        return [
            remote(
                og.at[b, :, pl.ds(p * width, width)],
                og.at[b, :, pl.ds(p * width, width)],
                a_send.at[slot, p],
                a_recv.at[slot, p],
                c,
                dst_tp,
            )
            for p in range(pieces)
        ]

    def turned(b, slot, j, h):
        return remote(
            og.at[b, :, pl.ds(pl.multiple_of(j * block + (base + h) * share, share), share)],
            og_t.at[base + h, c],
            t_send.at[slot, j, h],
            t_recv.at[c],
            per * b + j,
            base + h,
        )

    def start_turned(b, slot, j):
        @pl.when(per * b + j != c)
        def _():
            for h in range(2):
                turned(b, slot, j, h).start()

    to_far = block_copies(t, 0, far)
    to_sib = block_copies(t, 1, sib)
    for cp in to_far:
        cp.start()
    for cp in to_sib:
        cp.start()

    lax.fori_loop(0, modes, first_states, 0)
    st1[c] = rows[: 2 * modes, :].astype(BF16)

    def e_copy(d):
        return remote(
            st1.at[c], st1.at[c], e_send.at[d], e_recv.at[d], (c + d) % n_ctx, t
        )

    def each_peer(action):
        def step(d, carry):
            action(d)
            return carry

        lax.fori_loop(1, n_ctx, step, 0)

    each_peer(lambda d: e_copy(d).start())
    for j in range(per):
        start_turned(t, 0, j)

    def e_wait(d):
        slot = (c + n_ctx - d) % n_ctx
        remote(st1.at[slot], st1.at[slot], e_send.at[d], e_recv.at[d], c, t).wait_recv()

    each_peer(e_wait)

    q_dev = tab_ref[2 * modes : 3 * modes, :]

    def chain(k, carry):
        x, xp = carry
        block_state = st1[k].astype(F32)
        keep = k < c
        xp_new = q_dev * (xp + (1.0 * n_rows) * x) + block_state[modes:]
        x_new = q_dev * x + block_state[:modes]
        return jnp.where(keep, x_new, x), jnp.where(keep, xp_new, xp)

    zero = jnp.zeros((modes, chans), F32)
    x_in_state, xp_in_state = lax.fori_loop(0, n_ctx, chain, (zero, zero))
    rows[:modes, :] = x_in_state
    rows[modes : 2 * modes, :] = xp_in_state
    offset = (place * steps).astype(F32)

    def second(n, carry):
        a = jnp.broadcast_to(table(0, n), (SUB, chans))
        gain = jnp.broadcast_to(table(3, n), (SUB, chans))
        fade = jnp.exp(-offset * table(4, n))
        x0 = rows[pl.ds(n, 1), :]
        xp0 = rows[pl.ds(modes + n, 1), :]
        x = pre[n] + fade * x0
        xp = pre2[n] + fade * (xp0 + offset * x0)
        pre[n] = x
        pre2[n] = xp
        out = []
        for i in range(steps):
            x = a * x + u_sub[i]
            out.append(carry[i] + gain * x)
        return tuple(out)

    ys = lax.fori_loop(
        0, modes, second, tuple(jnp.zeros((SUB, chans), F32) for _ in range(steps))
    )
    y_ref[...] = gathered(ys) + skip_ref[...] * u_ref[...]

    res_all[c] = (outer_ref[...].astype(F32) * y_ref[...]).astype(BF16)

    def r_copy(d):
        return remote(
            res_all.at[c], res_all.at[c], r_send.at[d], r_recv.at[d], (c + d) % n_ctx, t
        )

    each_peer(lambda d: r_copy(d).start())

    w_copy.wait()
    tile = min(512, feats)

    def project(dest, sink):
        def step(k, carry):
            col = pl.multiple_of(k * tile, tile)
            part = jnp.dot(
                res_all[c],
                w_ref[:, pl.ds(pl.multiple_of(dest * feats + col, tile), tile)],
                preferred_element_type=F32,
            )
            sink[:, pl.ds(col, tile)] = part.astype(sink.dtype)
            return carry

        lax.fori_loop(0, feats // tile, step, 0)

    m_sib = [
        remote(sib_out.at[k], sib_in.at[k], m_send.at[k], m_recv.at[k], c, sib) for k in range(2)
    ]
    m_far = remote(x_out, x_in, m_send.at[2], m_recv.at[2], c, far)

    project(far_sib, sib_out.at[0])
    m_sib[0].start()
    project(far, d_cross)

    far_in = block_copies(far, 0, far)
    fwd = block_copies(far, 2, sib)
    for p in range(pieces):
        far_in[p].wait_recv()
        fwd[p].start()
        start_turned(far, 1, p)

    m_sib[0].wait_recv()
    x_out[...] = (d_cross[...] + sib_in[0].astype(F32)).astype(BF16)
    m_far.start()

    project(sib, sib_out.at[1])
    m_sib[1].start()
    project(t, d_own)

    for p in range(pieces):
        block_copies(sib, 1, sib)[p].wait_recv()
    for p in range(pieces):
        block_copies(far_sib, 2, sib)[p].wait_recv()

    gg_ref[...] = jnp.zeros_like(gg_ref)

    def back_project(b, carry):
        for k in range(feats // tile):
            gg_ref[...] += lax.dot_general(
                og[b, :, pl.ds(k * tile, tile)],
                w_ref[:, pl.ds(pl.multiple_of(b * feats + k * tile, tile), tile)],
                (((1,), (1,)), ((), ())),
                preferred_element_type=F32,
            )
        return carry

    lax.fori_loop(0, n_tp, back_project, 0)
    gc_ref[...] = gg_ref[...] * outer_ref[...].astype(F32)
    gouter_ref[...] = (gg_ref[...] * y_ref[...]).astype(BF16)

    spread(gc_ref[...], gc_sub)

    def third(n, carry):
        a = jnp.broadcast_to(table(0, n), (SUB, chans))
        q = jnp.broadcast_to(table(1, n), (SUB, chans))
        x = pre[n]
        xp = pre2[n]
        sum_a = jnp.zeros((SUB, chans), F32)
        sum_b = jnp.zeros((SUB, chans), F32)
        w = jnp.zeros((SUB, chans), F32)
        for i in range(steps):
            g = gc_sub[i]
            xp = a * (xp + x)
            x = a * x + u_sub[i]
            sum_a = sum_a + g * x
            sum_b = sum_b + g * xp
            w = a * w + gc_sub[steps - 1 - i]
        k = 1
        while k < SUB:
            w = w + q * up(w, k)
            q = q * q
            k *= 2
        pre[n] = up(w, 1)
        rows[pl.ds(n, 1), :] = w[:1]
        rows[pl.ds(modes + n, 1), :] = jnp.sum(sum_a, axis=0, keepdims=True)
        rows[pl.ds(2 * modes + n, 1), :] = jnp.sum(sum_b, axis=0, keepdims=True)
        return carry

    lax.fori_loop(0, modes, third, 0)
    rows[3 * modes :, :] = jnp.broadcast_to(
        jnp.sum(gc_ref[...] * u_ref[...], axis=0, keepdims=True), (modes, chans)
    )
    st2[c] = rows[...].astype(BF16)

    def g_copy(d):
        return remote(
            st2.at[c], st2.at[c], g_send.at[d], g_recv.at[d], (c + d) % n_ctx, t
        )

    each_peer(lambda d: g_copy(d).start())

    own_b = c // per
    own_j = c % per
    for h in range(n_tp):
        og_t[h, c] = og[own_b, :, pl.ds(pl.multiple_of(own_j * block + h * share, share), share)]

    def f_copy(way, slot, h, dest):
        return remote(
            og_t.at[h, slot],
            og_t.at[h, slot],
            f_send.at[way, slot],
            f_recv.at[way, slot],
            c,
            dest,
        )

    def pass_on(d):
        slot = (c + n_ctx - d) % n_ctx
        remote(
            og_t.at[t, slot], og_t.at[t, slot], t_send.at[0, 0, 0], t_recv.at[slot], c, t
        ).wait_recv()
        f_copy(0, slot, t, far).start()
        f_copy(1, slot, t, sib).start()

    each_peer(pass_on)

    m_sib[1].wait_recv()
    d_own[...] += sib_in[1].astype(F32)
    m_far.wait_recv()
    mixed_ref[...] = (d_own[...] + x_in[...].astype(F32)).astype(BF16)

    def r_wait(d):
        slot = (c + n_ctx - d) % n_ctx
        remote(
            res_all.at[slot], res_all.at[slot], r_send.at[d], r_recv.at[d], c, t
        ).wait_recv()

    each_peer(r_wait)

    def weigh(h):
        left = res_all[...].reshape(n_ctx * n_rows, chans)
        right = og_t[h].reshape(n_ctx * n_rows, share)
        gweight_ref[:, pl.ds(pl.multiple_of(h * share, share), share)] = lax.dot_general(
            left, right, (((0,), (0,)), ((), ())), preferred_element_type=F32
        )

    weigh(t)

    def pass_far(d):
        slot = (c + n_ctx - d) % n_ctx
        f_copy(0, slot, far, far).wait_recv()
        f_copy(2, slot, far, sib).start()

    each_peer(pass_far)

    def g_wait(d):
        slot = (c + n_ctx - d) % n_ctx
        remote(st2.at[slot], st2.at[slot], g_send.at[d], g_recv.at[d], c, t).wait_recv()

    each_peer(g_wait)

    def chain_back(k, carry):
        w, total = carry
        dev = n_ctx - 1 - k
        state = st2[dev].astype(F32)
        return (
            jnp.where(dev > c, q_dev * w + state[:modes], w),
            total + state[modes:],
        )

    w_state, total = lax.fori_loop(
        0, n_ctx, chain_back, (zero, jnp.zeros((3 * modes, chans), F32))
    )
    rows[:modes, :] = w_state
    gres_ref[...] = tab_ref[5 * modes : 6 * modes, :] * total[:modes]
    gdec_ref[...] = (
        tab_ref[6 * modes : 7 * modes, :] * total[:modes]
        - tab_ref[7 * modes :, :] * total[modes : 2 * modes]
    )
    gskip_ref[...] = total[2 * modes : 2 * modes + 1]

    back_offset = ((SUB - 1 - place) * steps).astype(F32)

    def fourth(n, carry):
        a = jnp.broadcast_to(table(0, n), (SUB, chans))
        gain = jnp.broadcast_to(table(3, n), (SUB, chans))
        w = pre[n] + jnp.exp(-back_offset * table(4, n)) * rows[pl.ds(n, 1), :]
        out = []
        for i in range(steps):
            w = a * w + gc_sub[steps - 1 - i]
            out.append(carry[i] + gain * w)
        return tuple(out)

    ws = lax.fori_loop(
        0, modes, fourth, tuple(jnp.zeros((SUB, chans), F32) for _ in range(steps))
    )
    y_ref[...] = gathered(ws[::-1]) + skip_ref[...] * gc_ref[...]
    ginner_ref[...] = (y_ref[...] * value_ref[...].astype(F32)).astype(BF16)
    gvalue_ref[...] = (y_ref[...] * inner_ref[...].astype(F32)).astype(BF16)

    weigh(far)

    def f_wait(way, h):
        def step(d):
            slot = (c + n_ctx - d) % n_ctx
            f_copy(way, slot, h, sib).wait_recv()

        return step

    each_peer(f_wait(1, sib))
    weigh(sib)
    each_peer(f_wait(2, far_sib))
    weigh(far_sib)

    for cp in to_far + to_sib + fwd:
        cp.wait_send()
    for slot, b in enumerate((t, far)):
        for j in range(per):

            @pl.when(per * b + j != c)
            def _():
                for h in range(2):
                    turned(b, slot, j, h).wait_send()

    def sent(d):
        slot = (c + n_ctx - d) % n_ctx
        f_copy(0, slot, t, far).wait_send()
        f_copy(1, slot, t, sib).wait_send()
        f_copy(2, slot, far, sib).wait_send()
        e_copy(d).wait_send()
        r_copy(d).wait_send()
        g_copy(d).wait_send()

    each_peer(sent)
    for cp in m_sib + [m_far]:
        cp.wait_send()


def hand_over(*refs):
    count = len(refs) // 3
    ins, outs, held = refs[:count], refs[count : 2 * count], refs[2 * count : 3 * count]
    in_sem, out_sem = refs[3 * count :]
    loads = [pltpu.make_async_copy(ins[k], held[k], in_sem.at[k]) for k in range(count)]
    stores = [pltpu.make_async_copy(held[k], outs[k], out_sem.at[k]) for k in range(count)]
    for cp in loads:
        cp.start()
    for k in range(count):
        loads[k].wait()
        stores[k].start()
    for cp in stores:
        cp.wait()


def fused_body(
    n_ctx, n_tp, outer_gate, inner_gate, values, residues, log_decay, skip_gain, out_weight, out_grad
):
    n_rows, chans = outer_gate.shape
    feats = out_grad.shape[1]
    modes = residues.shape[0]
    steps = n_rows // SUB
    block = feats * n_tp // n_ctx
    per = n_ctx // n_tp
    whole = pl.BlockSpec(memory_space=pl.ANY)
    hbm = pl.BlockSpec(memory_space=pltpu.HBM)
    vmem = pl.BlockSpec(memory_space=pltpu.VMEM)
    dma = pltpu.SemaphoreType.DMA
    outs = pl.pallas_call(
        functools.partial(fused_kernel, n_ctx, n_tp),
        out_shape=(
            jax.ShapeDtypeStruct((n_rows, feats), BF16),
            jax.ShapeDtypeStruct((n_rows, chans), BF16),
            jax.ShapeDtypeStruct((n_rows, chans), BF16),
            jax.ShapeDtypeStruct((n_rows, chans), BF16),
            jax.ShapeDtypeStruct((chans, block), F32),
            jax.ShapeDtypeStruct((1, chans), F32),
            jax.ShapeDtypeStruct((modes, chans), F32),
            jax.ShapeDtypeStruct((modes, chans), F32),
        ),
        in_specs=[hbm] * 8,
        out_specs=(vmem,) * 8,
        scratch_shapes=[
            pltpu.VMEM((n_rows, chans), BF16),
            pltpu.VMEM((n_rows, chans), BF16),
            pltpu.VMEM((n_rows, chans), BF16),
            pltpu.VMEM((2, modes, chans), F32),
            pltpu.VMEM((1, chans), F32),
            pltpu.VMEM((8 * modes, chans), F32),
            pltpu.VMEM(out_weight.shape, BF16),
            pltpu.VMEM((n_tp, n_rows, feats), BF16),
            pltpu.VMEM((n_tp, n_ctx, n_rows, block // n_tp), BF16),
            pltpu.VMEM((n_ctx, n_rows, chans), BF16),
            pltpu.VMEM((n_ctx, 2 * modes, chans), BF16),
            pltpu.VMEM((n_ctx, 4 * modes, chans), BF16),
            pltpu.VMEM((n_rows, feats), F32),
            pltpu.VMEM((n_rows, feats), F32),
            pltpu.VMEM((2, n_rows, feats), BF16),
            pltpu.VMEM((2, n_rows, feats), BF16),
            pltpu.VMEM((n_rows, feats), BF16),
            pltpu.VMEM((n_rows, feats), BF16),
            pltpu.VMEM((n_rows, chans), F32),
            pltpu.VMEM((n_rows, chans), F32),
            pltpu.VMEM((n_rows, chans), F32),
            pltpu.VMEM((n_rows, chans), F32),
            pltpu.VMEM((chans // 128, n_rows, 128), F32),
            pltpu.VMEM((steps, SUB, chans), F32),
            pltpu.VMEM((steps, SUB, chans), F32),
            pltpu.VMEM((4 * modes, chans), F32),
            pltpu.VMEM((modes, SUB, chans), F32),
            pltpu.VMEM((modes, SUB, chans), F32),
            dma((7,)),
            dma,
            dma((3, per)),
            dma((3, per)),
            dma((2, per, 2)),
            dma((n_ctx,)),
            dma((3, n_ctx)),
            dma((3, n_ctx)),
            dma((n_ctx,)),
            dma((n_ctx,)),
            dma((n_ctx,)),
            dma((n_ctx,)),
            dma((n_ctx,)),
            dma((n_ctx,)),
            dma((3,)),
            dma((3,)),
        ],
        compiler_params=pltpu.CompilerParams(
            collective_id=0, has_side_effects=True, vmem_limit_bytes=60 * 2**20
        ),
    )(
        outer_gate, inner_gate, values, residues, log_decay, skip_gain[None, :], out_weight, out_grad
    )
    outs = pl.pallas_call(
        hand_over,
        out_shape=tuple(jax.ShapeDtypeStruct(o.shape, o.dtype) for o in outs),
        in_specs=[whole] * 8,
        out_specs=(whole,) * 8,
        scratch_shapes=[pltpu.VMEM(o.shape, o.dtype) for o in outs] + [dma((8,)), dma((8,))],
        compiler_params=pltpu.CompilerParams(vmem_limit_bytes=60 * 2**20),
    )(*outs)
    return outs[:5] + (outs[5][0],) + outs[6:]


def body(n_ctx, n_tp, *arrays):
    n_rows = arrays[0].shape[0]
    feats = arrays[-1].shape[1]
    modes = arrays[3].shape[0]
    pairs = n_tp == 4 and n_ctx % n_tp == 0 and (feats * n_tp // n_ctx) % (128 * n_tp) == 0
    if pairs and n_rows % 16 == 0 and modes % 16 == 0:
        return fused_body(n_ctx, n_tp, *arrays)
    return spectral_body(*arrays)


def solution(mesh):
    placed = (
        P("ctx", "tp"),
        P("ctx", "tp"),
        P("ctx", "tp"),
        P(None, "tp"),
        P(None, "tp"),
        P("tp"),
        P("tp", None),
        P("ctx", "tp"),
    )
    return jax.shard_map(
        functools.partial(body, mesh.shape["ctx"], mesh.shape["tp"]),
        mesh=mesh,
        in_specs=placed,
        out_specs=(
            P("ctx", "tp"),
            P("ctx", "tp"),
            P("ctx", "tp"),
            P("ctx", "tp"),
            P("tp", "ctx"),
            P("tp"),
            P(None, "tp"),
            P(None, "tp"),
        ),
        check_vma=False,
    )
```
